32 devices in a mesh: row: 4 (over y, x), col: 8 (over z, core).
Axes of the slice: x: 2, y: 2, z: 4, core: 2. Of those that a mesh axis runs over, the one named last changes fastest.
Arguments:
- row_ids: int32 [32], P('row'), may hold values from -1 to 31, as said below
- a_tiles: bfloat16 [2048, 1024], P('row', 'col'), may hold values from -6 to 6
- a_mask: int32 [32, 16], P('row', 'col'), may hold values 0 or 1
- b_tiles: bfloat16 [1024, 6144], P('row', 'col'), may hold values from -0.375 to 0.375
- b_mask: int32 [16, 96], P('row', 'col'), may hold values 0 or 1
- c_keep: int32 [32, 96], P(None, 'col'), may hold values 0 or 1
Outputs:
- product_out: bfloat16 [2048, 6144], P('row', 'col')
The draws below stay inside these ranges and needn't reach their ends.
Inputs may be any that keep to these rules, and one draw needn't show every extreme that they name: `row_ids`: within a group of 8 slots the live ids come first and -1 fills the rest; live ids are distinct over all slots; every group has at least half of its slots live and some group has all 8 live.
All inputs are finite; a program needn't handle non-finite values. No bound on the sum of `a_mask` or of `b_mask` or of `c_keep` on one device may be relied on, other than what follows from the above.
Results may differ from the reference program's by a relative error of at most 0.001.
Values may be sent and summed in bfloat16 or wider, within the bound.
No kernel may reach another device: no remote copies, remote signals or barrier semaphores. Data moves between devices by JAX's collectives and lax.ppermute only.
A program may use at most 64 MiB of HBM per device.

```python
import jax
import jax.numpy as jnp
from jax import lax

TILE = 64
KB = 2
CB = 12
S = 8
GROUPS = 4
PANELS = 8


def draw_row_ids(key, part):
    first_key, second_key, third_key = jax.random.split(key, 3)
    counts = jax.random.randint(first_key, (GROUPS,), (S + 1) // 2, S + 1)
    full_group = jax.random.randint(second_key, (), 0, GROUPS)
    counts = jnp.where(jnp.arange(GROUPS, dtype=jnp.int32) == full_group, S, counts)
    shuffled = jax.random.permutation(third_key, GROUPS * S).astype(jnp.int32)
    positions = jnp.arange(GROUPS * S, dtype=jnp.int32)
    within = positions % S
    owner = positions // S
    return jnp.where(within < counts[owner], shuffled, -1).astype(jnp.int32)


def set_ends(array, key, least, largest):
    place = [jax.random.randint(jax.random.fold_in(key, axis), (), 0, length) for axis, length in enumerate(array.shape)]
    longest = array.shape.index(max(array.shape))
    neighbour = place[:longest] + [(place[longest] + 1) % array.shape[longest]] + place[longest + 1:]
    return array.at[tuple(place)].set(least).at[tuple(neighbour)].set(largest)


def block_scale(stream_key, dims, cuts, low, high):
    loudness = 1.0
    for position, parts in cuts:
        heights = jax.random.uniform(jax.random.fold_in(jax.random.fold_in(stream_key, 6), position), (parts,), jnp.float32, low / len(cuts), high / len(cuts))
        loudness = loudness * jnp.repeat(jnp.exp(heights), dims[position] // parts).reshape((-1,) + (1,) * (len(dims) - 1 - position))
    return loudness


def normal_values(key, dims, width, limit, cuts=(), kind=jnp.bfloat16):
    array = width * jax.random.normal(key, dims, jnp.float32)
    if cuts:
        array = array * block_scale(key, dims, cuts, -0.22, 0.18)
    return jnp.clip(array, -limit, limit).astype(kind)


def setup_inputs(seed: int = 0) -> dict:
    key_list = jax.random.split(jax.random.key(seed), 7)
    return {
        "row_ids": draw_row_ids(jax.random.fold_in(key_list[6], 71), 0),
        "a_tiles": normal_values(key_list[1], (GROUPS * S * TILE, PANELS * KB * TILE), 1.0, 6.0, ((0, 4), (1, 8))),
        "a_mask": set_ends((jax.random.randint(key_list[2], (GROUPS * S, PANELS * KB), 0, 2) < 1).astype(jnp.int32), jax.random.fold_in(key_list[2], 1), 0, 1),
        "b_tiles": normal_values(key_list[3], (PANELS * KB * TILE, PANELS * CB * TILE), (PANELS * KB * TILE // 4) ** -0.5, 0.375, ((0, 4), (1, 8))),
        "b_mask": set_ends((jax.random.randint(key_list[4], (PANELS * KB, PANELS * CB), 0, 2) < 1).astype(jnp.int32), jax.random.fold_in(key_list[4], 1), 0, 1),
        "c_keep": set_ends((jax.random.randint(key_list[5], (GROUPS * S, PANELS * CB), 0, 4) < 3).astype(jnp.int32), jax.random.fold_in(key_list[5], 1), 0, 1),
    }


def reference(row_ids, a_tiles, a_mask, b_tiles, b_mask, c_keep):
    ratio_cols = PANELS // GROUPS
    panel_width = KB * TILE
    a_masked = a_tiles.reshape(GROUPS * S, TILE, PANELS * KB, TILE) * a_mask.astype(jnp.bfloat16)[:, None, :, None]
    a_masked = a_masked.reshape(GROUPS, S * TILE, PANELS, panel_width)
    b_masked = b_tiles.reshape(PANELS * KB, TILE, PANELS * CB, TILE) * b_mask.astype(jnp.bfloat16)[:, None, :, None]
    b_masked = b_masked.reshape(PANELS, panel_width, PANELS, CB * TILE)
    col_shift = jnp.arange(PANELS, dtype=jnp.int32)
    b_inner = jax.vmap(lambda block_cols, shift_by: jnp.roll(block_cols, shift_by, axis=0), in_axes=(2, 0), out_axes=2)(b_masked, col_shift)
    b_inner = b_inner.reshape(PANELS * panel_width, PANELS * CB * TILE)
    clipped = jnp.maximum(row_ids, 0).astype(jnp.int32)
    keep = jnp.where(row_ids[:, None] >= 0, c_keep[clipped].astype(jnp.float32), jnp.zeros((), jnp.float32))
    keep = keep.reshape(GROUPS, S, PANELS * CB)

    def one_group(inputs):
        group_rows, group_index, group_keep = inputs
        a_inner = jnp.roll(group_rows, ratio_cols * group_index + ratio_cols - 1, axis=1)
        a_inner = a_inner.reshape(S * TILE, PANELS * panel_width)
        product = jnp.dot(a_inner, b_inner, preferred_element_type=jnp.float32)
        masked = product.reshape(S, TILE, PANELS * CB, TILE) * group_keep[:, None, :, None]
        return masked.reshape(S * TILE, PANELS * CB * TILE).astype(jnp.bfloat16)

    result = lax.map(one_group, (a_masked, jnp.arange(GROUPS, dtype=jnp.int32), keep))
    return result.reshape(GROUPS * S * TILE, PANELS * CB * TILE)
```

```python
import functools

import jax
import jax.numpy as jnp
from jax import lax
from jax.experimental import pallas as pl
from jax.experimental.pallas import tpu as pltpu
from jax.sharding import PartitionSpec as P

TILE = 64
ANY = pl.BlockSpec(memory_space=pl.ANY)
VMEM = pl.BlockSpec(memory_space=pltpu.VMEM)
SMEM = pl.BlockSpec(memory_space=pltpu.SMEM)


def spread_matrix(blocks):
    shape = (blocks, blocks * TILE)
    owner = lax.broadcasted_iota(jnp.int32, shape, 1) // TILE
    return (owner == lax.broadcasted_iota(jnp.int32, shape, 0)).astype(jnp.float32)


def spread(mask):
    return jnp.dot(
        mask.astype(jnp.float32), spread_matrix(mask.shape[1]), preferred_element_type=jnp.float32
    )


def mask_kernel(parts, mask_ref, tiles_ref, *out_refs):
    wide = spread(mask_ref[...]).astype(jnp.bfloat16)
    rows = tiles_ref.shape[0] // parts
    for part, out_ref in enumerate(out_refs):
        for i in range(rows // TILE):
            block = (part * rows) // TILE + i
            source = pl.ds(block * TILE, TILE)
            out_ref[pl.ds(i * TILE, TILE), :] = tiles_ref[source, :] * wide[block : block + 1, :]


def masked(mask, tiles, parts):
    part = jax.ShapeDtypeStruct((tiles.shape[0] // parts, tiles.shape[1]), tiles.dtype)
    return pl.pallas_call(
        functools.partial(mask_kernel, parts),
        out_shape=(part,) * parts,
        in_specs=[VMEM, VMEM],
        out_specs=(VMEM,) * parts,
        cost_estimate=pl.CostEstimate(
            flops=tiles.size, bytes_accessed=4 * tiles.size, transcendentals=0
        ),
    )(mask, tiles)


def product_kernel(
    a_sources, b_pieces, mesh_sizes, row_ids_ref, c_keep_ref, *refs
):
    row_count, col_count = mesh_sizes
    ratio = col_count // row_count
    a_refs = refs[: len(a_sources)]
    b_refs = refs[len(a_sources) : len(a_sources) + len(b_pieces)]
    out_ref, a_all, b_all, out_tile, keep_wide, in_sem, out_sem = refs[
        len(a_sources) + len(b_pieces) :
    ]
    me_row, me_col = lax.axis_index("row"), lax.axis_index("col")
    width = a_all.shape[1] // col_count
    copies = []
    for distance, a_ref in zip(a_sources, a_refs, strict=True):
        stored = me_col ^ distance
        inner = lax.rem(stored + ratio * me_row + ratio - 1, col_count)
        columns = pl.ds(pl.multiple_of(inner * width, width), width)
        copies.append((a_ref, a_all.at[:, columns]))
    for (distance, first), b_ref in zip(b_pieces, b_refs, strict=True):
        piece = min(width, b_ref.shape[0])
        for start in range(0, b_ref.shape[0], piece):
            place = first + start
            stored = (me_row ^ distance) * ratio + place // width
            inner = lax.rem(stored + me_col, col_count)
            rows = pl.ds(pl.multiple_of(inner * width + place % width, piece), piece)
            copies.append((b_ref.at[pl.ds(start, piece), :], b_all.at[rows, :]))
    copies = [
        pltpu.make_async_copy(source, target, in_sem.at[i])
        for i, (source, target) in enumerate(copies)
    ]
    for copy in copies:
        copy.start()

    rows_live = row_ids_ref[...]
    which = lax.broadcasted_iota(jnp.int32, (rows_live.shape[0], c_keep_ref.shape[0]), 1)
    onehot = (rows_live == which).astype(jnp.float32)
    keep = jnp.dot(
        onehot, c_keep_ref[...].astype(jnp.float32), preferred_element_type=jnp.float32
    )
    keep_wide[...] = spread(keep)

    for copy in copies:
        copy.wait()
    rows = out_tile.shape[1]
    writes = []
    for step in range(a_all.shape[0] // rows):
        total = jnp.dot(
            a_all[pl.ds(step * rows, rows), :], b_all[...], preferred_element_type=jnp.float32
        )
        for i in range(rows // TILE):
            slot = step * rows // TILE + i
            out_tile[step, pl.ds(i * TILE, TILE), :] = (
                total[i * TILE : (i + 1) * TILE] * keep_wide[pl.ds(slot, 1), :]
            ).astype(jnp.bfloat16)
        writes.append(
            pltpu.make_async_copy(
                out_tile.at[step], out_ref.at[pl.ds(step * rows, rows), :], out_sem.at[step]
            )
        )
        writes[-1].start()
    for write in writes:
        write.wait()


def product(row_ids, c_keep, a_blocks, b_blocks, mesh_sizes):
    a_rows, width = a_blocks[0].shape
    columns = next(iter(b_blocks.values())).shape[1]
    inner = width * mesh_sizes[1]
    rows = 2 * TILE
    steps = a_rows // rows
    n_copies = len(a_blocks) + sum(-(-b.shape[0] // width) for b in b_blocks.values())
    return pl.pallas_call(
        functools.partial(product_kernel, tuple(a_blocks), tuple(b_blocks), mesh_sizes),
        out_shape=jax.ShapeDtypeStruct((a_rows, columns), jnp.bfloat16),
        in_specs=[VMEM, VMEM] + [ANY] * (len(a_blocks) + len(b_blocks)),
        out_specs=ANY,
        scratch_shapes=[
            pltpu.VMEM((a_rows, inner), jnp.bfloat16),
            pltpu.VMEM((inner, columns), jnp.bfloat16),
            pltpu.VMEM((steps, rows, columns), jnp.bfloat16),
            pltpu.VMEM((a_rows // TILE, columns), jnp.float32),
            pltpu.SemaphoreType.DMA((n_copies,)),
            pltpu.SemaphoreType.DMA((steps,)),
        ],
        compiler_params=pltpu.CompilerParams(vmem_limit_bytes=32 * 1024 * 1024),
        cost_estimate=pl.CostEstimate(
            flops=2 * a_rows * inner * columns,
            bytes_accessed=2 * (a_rows * inner + inner * columns + a_rows * columns),
            transcendentals=0,
        ),
    )(row_ids[:, None], c_keep, *a_blocks.values(), *b_blocks.values())


def swapped(block, axis, distance):
    return lax.ppermute(block, axis, [(i, i ^ distance) for i in range(lax.axis_size(axis))])


def gathered_b(b_eff):
    row_count = lax.axis_size("row")
    rows = b_eff.shape[0]
    half = rows // 2
    if row_count != 4:
        pieces = {(d, 0): swapped(b_eff, "row", d) for d in range(1, row_count)}
        return {(0, 0): b_eff, **pieces}
    near, far = swapped(b_eff, "row", 1), swapped(b_eff, "row", 2)
    return {
        (0, 0): b_eff,
        (1, 0): near,
        (2, 0): far,
        (3, 0): swapped(near[:half], "row", 2),
        (3, half): swapped(far[half:], "row", 1),
    }


def gathered_a(a_eff):
    blocks = {0: a_eff}
    for distance in range(2, lax.axis_size("col"), 2):
        blocks[distance] = swapped(a_eff, "col", distance)
    for distance in tuple(blocks):
        blocks[distance + 1] = swapped(blocks[distance], "col", 1)
    return blocks


def per_device(row_ids, a_tiles, a_mask, b_tiles, b_mask, c_keep):
    (b_eff,) = masked(b_mask, b_tiles, 1)
    (a_eff,) = masked(a_mask, a_tiles, 1)
    return product(
        row_ids,
        c_keep,
        gathered_a(a_eff),
        gathered_b(b_eff),
        (lax.axis_size("row"), lax.axis_size("col")),
    )


def solution(mesh):
    placed = (
        P("row"),
        P("row", "col"),
        P("row", "col"),
        P("row", "col"),
        P("row", "col"),
        P(None, "col"),
    )
    return jax.shard_map(
        per_device, mesh=mesh, in_specs=placed, out_specs=P("row", "col"), check_vma=False
    )
```

```python
import functools

import jax
import jax.numpy as jnp
from jax import lax
from jax.experimental import pallas as pl
from jax.experimental.pallas import tpu as pltpu
from jax.sharding import PartitionSpec as P

TILE = 64
ANY = pl.BlockSpec(memory_space=pl.ANY)
VMEM = pl.BlockSpec(memory_space=pltpu.VMEM)
SMEM = pl.BlockSpec(memory_space=pltpu.SMEM)


def near(array):
    return pltpu.with_memory_space_constraint(array, pltpu.VMEM)


def keep_present(mask_at, tiles_ref, out_ref):
    shape = (TILE, 2 * TILE)
    lane = lax.broadcasted_iota(jnp.int32, shape, 1)
    for i in range(tiles_ref.shape[0] // TILE):
        for j in range(0, tiles_ref.shape[1] // TILE, 2):
            place = (pl.ds(i * TILE, TILE), pl.ds(j * TILE, 2 * TILE))
            present = jnp.where(lane < TILE, mask_at(i, j), mask_at(i, j + 1)) != 0
            tiles = tiles_ref[place]
            out_ref[place] = jnp.where(present, tiles, jnp.zeros_like(tiles))


def mask_kernel(a_mask_ref, b_mask_ref, a_ref, b_ref, a_out_ref, b_out_ref):
    keep_present(lambda i, j: b_mask_ref[i, j], b_ref, b_out_ref)
    keep_present(lambda i, j: a_mask_ref[j, i], a_ref, a_out_ref)


def masked(a_tiles, a_mask, b_tiles, b_mask):
    return pl.pallas_call(
        mask_kernel,
        out_shape=(
            pltpu.VMEM(a_tiles.shape, a_tiles.dtype),
            pltpu.VMEM(b_tiles.shape, b_tiles.dtype),
        ),
        in_specs=[SMEM, SMEM, VMEM, VMEM],
        out_specs=(VMEM, VMEM),
        cost_estimate=pl.CostEstimate(
            flops=a_tiles.size + b_tiles.size,
            bytes_accessed=4 * (a_tiles.size + b_tiles.size),
            transcendentals=0,
        ),
    )(a_mask.T, b_mask, a_tiles, b_tiles)


def spread(mask):
    shape = (mask.shape[1], mask.shape[1] * TILE)
    owner = lax.broadcasted_iota(jnp.int32, shape, 1) // TILE
    ones = (owner == lax.broadcasted_iota(jnp.int32, shape, 0)).astype(jnp.float32)
    return jnp.dot(mask, ones, preferred_element_type=jnp.float32)


def early_kernel(b_distances, mesh_sizes, *refs):
    row_count, col_count = mesh_sizes
    ratio = col_count // row_count
    a_refs, refs = refs[:4], refs[4:]
    b_refs, (total_ref, a_last_ref, a_all) = refs[: row_count - 1], refs[row_count - 1 :]
    me_row, me_col = lax.axis_index("row"), lax.axis_index("col")
    width = a_all.shape[1] // col_count
    depth = ratio * width

    for distance in range(col_count):
        far, chip = divmod(distance // 2, col_count // 4)
        a_ref = a_refs[distance % 2 * 2 + far]
        block = pl.ds(chip * width, width)
        shift = (me_col ^ distance) - me_col
        stored = lax.rem(shift + ratio * me_row + ratio - 1 + 2 * col_count, col_count)
        a_all[:, pl.ds(pl.multiple_of(stored * width, width), width)] = a_ref[:, block]

    def a_columns(distance):
        return pl.ds(pl.multiple_of((me_row ^ distance) * depth, depth), depth)

    *distances, last = b_distances(me_col)
    a_last_ref[...] = a_all[:, a_columns(last)]
    for start in range(0, total_ref.shape[0], 2 * TILE):
        rows = pl.ds(start, 2 * TILE)
        total = None
        for distance, b_ref in zip(distances, b_refs, strict=True):
            term = jnp.dot(
                a_all[rows, a_columns(distance)], b_ref[...], preferred_element_type=jnp.float32
            )
            total = term if total is None else total + term
        total_ref[rows, :] = total


def early_product(a_blocks, b_blocks, b_distances, mesh_sizes):
    a_rows, half = a_blocks[0].shape
    depth, columns = b_blocks[0].shape
    inner = 4 * half
    return pl.pallas_call(
        functools.partial(early_kernel, b_distances, mesh_sizes),
        out_shape=(
            pltpu.VMEM((a_rows, columns), jnp.float32),
            pltpu.VMEM((a_rows, depth), jnp.bfloat16),
        ),
        in_specs=[VMEM] * (len(a_blocks) + len(b_blocks)),
        out_specs=(VMEM, VMEM),
        scratch_shapes=[pltpu.VMEM((a_rows, inner), jnp.bfloat16)],
        compiler_params=pltpu.CompilerParams(vmem_limit_bytes=24 * 1024 * 1024),
        cost_estimate=pl.CostEstimate(
            flops=2 * a_rows * (inner - depth) * columns,
            bytes_accessed=2 * (a_rows * inner + (inner - depth) * columns) + 4 * a_rows * columns,
            transcendentals=0,
        ),
    )(*(near(block) for block in (*a_blocks, *b_blocks)))


def last_kernel(row_ids_ref, c_keep_ref, total_ref, a_ref, b_ref, out_ref, out_tiles, out_sem):
    ids = row_ids_ref[...]
    which = lax.broadcasted_iota(jnp.int32, (ids.shape[0], c_keep_ref.shape[1]), 1)
    keep = spread(
        lax.dot_general(
            (ids == which).astype(jnp.float32),
            c_keep_ref[...].astype(jnp.float32),
            (((1,), (1,)), ((), ())),
            preferred_element_type=jnp.float32,
        )
    )
    rows = out_tiles.shape[1]
    writes = []
    for step in range(out_tiles.shape[0]):
        own = pl.ds(step * rows, rows)
        total = total_ref[own, :] + jnp.dot(
            a_ref[own, :], b_ref[...], preferred_element_type=jnp.float32
        )
        for i in range(rows // TILE):
            slot = step * rows // TILE + i
            out_tiles[step, pl.ds(i * TILE, TILE), :] = (
                total[i * TILE : (i + 1) * TILE] * keep[slot : slot + 1]
            ).astype(jnp.bfloat16)
        writes.append(pltpu.make_async_copy(out_tiles.at[step], out_ref.at[own, :], out_sem.at[step]))
        writes[-1].start()
    for write in writes:
        write.wait()


def last_product(row_ids, c_keep, total, a_last, b_last):
    a_rows, columns = total.shape
    rows = 2 * TILE
    steps = a_rows // rows
    return pl.pallas_call(
        last_kernel,
        out_shape=jax.ShapeDtypeStruct((a_rows, columns), jnp.bfloat16),
        in_specs=[VMEM] * 5,
        out_specs=ANY,
        scratch_shapes=[
            pltpu.VMEM((steps, rows, columns), jnp.bfloat16),
            pltpu.SemaphoreType.DMA((steps,)),
        ],
        compiler_params=pltpu.CompilerParams(vmem_limit_bytes=24 * 1024 * 1024),
        cost_estimate=pl.CostEstimate(
            flops=2 * a_rows * b_last.size,
            bytes_accessed=4 * total.size + 2 * (a_last.size + b_last.size + total.size),
            transcendentals=0,
        ),
    )(near(row_ids[:, None]), near(c_keep.T), near(total), near(a_last), near(b_last))


def swapped(block, axis, distance):
    return lax.ppermute(block, axis, [(i, i ^ distance) for i in range(lax.axis_size(axis))])


def crossed(block, even, odd):
    cols = lax.axis_size("col")
    pairs = [
        (r * cols + c, (r ^ (odd if c % 2 else even)) * cols + c)
        for r in range(lax.axis_size("row"))
        for c in range(cols)
    ]
    return lax.ppermute(block, ("row", "col"), pairs)


def gathered_b(b_eff):
    rows = lax.axis_size("row")
    if rows != 4:
        blocks = [b_eff] + [swapped(b_eff, "row", d) for d in range(1, rows)]
        return blocks, lambda col: tuple(range(rows))
    first = crossed(b_eff, 1, 2)
    second = crossed(b_eff, 2, 1)
    last = crossed(first, 2, 1)
    return [b_eff, first, second, last], lambda col: (0, 1 + (col & 1), 2 - (col & 1), 3)


def beside_kernel(*refs):
    *block_refs, out_ref = refs
    width = block_refs[0].shape[1]
    for i, block_ref in enumerate(block_refs):
        out_ref[:, i * width : (i + 1) * width] = block_ref[...]


def beside(blocks):
    rows, width = blocks[0].shape
    return pl.pallas_call(
        beside_kernel,
        out_shape=pltpu.VMEM((rows, width * len(blocks)), blocks[0].dtype),
        in_specs=[VMEM] * len(blocks),
        out_specs=VMEM,
        compiler_params=pltpu.CompilerParams(vmem_limit_bytes=24 * 1024 * 1024),
        cost_estimate=pl.CostEstimate(
            flops=0, bytes_accessed=4 * rows * width * len(blocks), transcendentals=0
        ),
    )(*(near(block) for block in blocks))


def gathered_a(a_eff):
    chips = [a_eff] + [swapped(a_eff, "col", d) for d in range(2, lax.axis_size("col"), 2)]
    middle = len(chips) // 2
    owns = [beside(chips[:middle]), beside(chips[middle:])]
    return owns + [swapped(own, "col", 1) for own in owns]


def per_device(row_ids, a_tiles, a_mask, b_tiles, b_mask, c_keep):
    a_eff, b_eff = masked(a_tiles, a_mask, b_tiles, b_mask)
    b_blocks, b_distances = gathered_b(b_eff)
    sizes = (lax.axis_size("row"), lax.axis_size("col"))
    total, a_last = early_product(gathered_a(a_eff), b_blocks[:-1], b_distances, sizes)
    return last_product(row_ids, c_keep, total, a_last, b_blocks[-1])


def solution(mesh):
    placed = (
        P("row"),
        P("row", "col"),
        P("row", "col"),
        P("row", "col"),
        P("row", "col"),
        P(None, "col"),
    )
    return jax.shard_map(
        per_device, mesh=mesh, in_specs=placed, out_specs=P("row", "col"), check_vma=False
    )
```

```python
import functools

import jax
import jax.numpy as jnp
from jax import lax
from jax.experimental import pallas as pl
from jax.experimental.pallas import tpu as pltpu
from jax.sharding import PartitionSpec as P

TILE = 64
ANY = pl.BlockSpec(memory_space=pl.ANY)
VMEM = pl.BlockSpec(memory_space=pltpu.VMEM)
SMEM = pl.BlockSpec(memory_space=pltpu.SMEM)
LIMITS = pltpu.CompilerParams(vmem_limit_bytes=24 * 1024 * 1024)


def near(array):
    return pltpu.with_memory_space_constraint(array, pltpu.VMEM)


def cost(flops, bytes_accessed):
    return pl.CostEstimate(flops=flops, bytes_accessed=bytes_accessed, transcendentals=0)


def keep_present(mask_at, tiles_ref, out_ref):
    lane = lax.broadcasted_iota(jnp.int32, (TILE, 2 * TILE), 1)
    for i in range(tiles_ref.shape[0] // TILE):
        for j in range(0, tiles_ref.shape[1] // TILE, 2):
            place = (pl.ds(i * TILE, TILE), pl.ds(j * TILE, 2 * TILE))
            present = jnp.where(lane < TILE, mask_at(i, j), mask_at(i, j + 1)) != 0
            tiles = tiles_ref[place]
            out_ref[place] = jnp.where(present, tiles, jnp.zeros_like(tiles))


def mask_kernel(a_mask_ref, b_mask_ref, a_ref, b_ref, a_out_ref, b_out_ref):
    keep_present(lambda i, j: b_mask_ref[i, j], b_ref, b_out_ref)
    keep_present(lambda i, j: a_mask_ref[j, i], a_ref, a_out_ref)


def masked(a_tiles, a_mask, b_tiles, b_mask):
    size = a_tiles.size + b_tiles.size
    return pl.pallas_call(
        mask_kernel,
        out_shape=(
            pltpu.VMEM(a_tiles.shape, a_tiles.dtype),
            pltpu.VMEM(b_tiles.shape, b_tiles.dtype),
        ),
        in_specs=[SMEM, SMEM, VMEM, VMEM],
        out_specs=(VMEM, VMEM),
        cost_estimate=cost(size, 4 * size),
    )(a_mask.T, b_mask, a_tiles, b_tiles)


def spread(mask):
    shape = (mask.shape[1], mask.shape[1] * TILE)
    owner = lax.broadcasted_iota(jnp.int32, shape, 1) // TILE
    ones = (owner == lax.broadcasted_iota(jnp.int32, shape, 0)).astype(jnp.float32)
    return jnp.dot(mask, ones, preferred_element_type=jnp.float32)


def put_in_order(b_place, mesh_sizes, width, groups, panels_ref):
    row_count, col_count = mesh_sizes
    ratio = col_count // row_count
    me_row, me_col = lax.axis_index("row"), lax.axis_index("col")
    for array_ref, distances in groups:
        for i, distance in enumerate(distances):
            shift = (me_col ^ distance) - me_col
            stored = lax.rem(shift + ratio * me_row + ratio - 1 + 2 * col_count, col_count)
            place = b_place((stored // ratio) ^ me_row)
            columns = pl.ds(pl.multiple_of(place * width, width), width)
            panels_ref[:, columns] = array_ref[:, i * width : (i + 1) * width]


def early_kernel(distances, b_place, mesh_sizes, row_ids_ref, c_keep_ref, *refs):
    a_refs, refs = refs[: len(distances)], refs[len(distances) :]
    early = mesh_sizes[0] - 1
    b_refs, (total_ref, a_last_ref, keep_ref, panels) = refs[:early], refs[early:]
    width = a_last_ref.shape[1]
    put_in_order(b_place, mesh_sizes, width, zip(a_refs, distances, strict=True), panels)
    a_last_ref[...] = panels[:, early * width :]
    second = jnp.concatenate([b_ref[width:, :] for b_ref in b_refs], axis=0)
    for start in range(0, total_ref.shape[0], 2 * TILE):
        rows = pl.ds(start, 2 * TILE)
        total_ref[rows, :] = jnp.dot(
            panels[rows, : early * width], second, preferred_element_type=jnp.float32
        )
    ids = row_ids_ref[...]
    which = lax.broadcasted_iota(jnp.int32, (ids.shape[0], c_keep_ref.shape[1]), 1)
    keep_ref[...] = spread(
        lax.dot_general(
            (ids == which).astype(jnp.float32),
            c_keep_ref[...].astype(jnp.float32),
            (((1,), (1,)), ((), ())),
            preferred_element_type=jnp.float32,
        )
    )


def early_product(row_ids, c_keep, a_groups, b_blocks, b_place, mesh_sizes):
    arrays, distances = zip(*a_groups, strict=True)
    a_rows = arrays[0].shape[0]
    depth, columns = b_blocks[0].shape
    width = depth // 2
    return pl.pallas_call(
        functools.partial(early_kernel, distances, b_place, mesh_sizes),
        out_shape=(
            pltpu.VMEM((a_rows, columns), jnp.float32),
            pltpu.VMEM((a_rows, width), jnp.bfloat16),
            pltpu.VMEM((row_ids.shape[0], columns), jnp.float32),
        ),
        in_specs=[VMEM] * (2 + len(arrays) + len(b_blocks)),
        out_specs=(VMEM, VMEM, VMEM),
        scratch_shapes=[pltpu.VMEM((a_rows, width * mesh_sizes[0]), jnp.bfloat16)],
        compiler_params=LIMITS,
        cost_estimate=cost(2 * a_rows * width * len(b_blocks) * columns, 4 * a_rows * columns),
    )(near(row_ids[:, None]), near(c_keep.T), *(near(block) for block in (*arrays, *b_blocks)))


def last_kernel(distances, b_place, mesh_sizes, keep_ref, total_ref, a_last_ref, *refs):
    row_count = mesh_sizes[0]
    a_refs, refs = refs[: len(distances)], refs[len(distances) :]
    b_refs, (out_ref, panels, out_tiles, out_sem) = refs[:row_count], refs[row_count:]
    width = a_last_ref.shape[1]
    put_in_order(b_place, mesh_sizes, width, zip(a_refs, distances, strict=True), panels)
    panels[:, row_count * width :] = a_last_ref[...]
    blocks = jnp.concatenate(
        [b_ref[:width, :] for b_ref in b_refs] + [b_refs[-1][width:, :]], axis=0
    )
    rows = out_tiles.shape[1]
    writes = []
    for step in range(out_tiles.shape[0]):
        own = pl.ds(step * rows, rows)
        total = total_ref[own, :] + jnp.dot(
            panels[own, :], blocks, preferred_element_type=jnp.float32
        )
        for i in range(rows // TILE):
            slot = step * rows // TILE + i
            out_tiles[step, pl.ds(i * TILE, TILE), :] = (
                total[i * TILE : (i + 1) * TILE] * keep_ref[slot : slot + 1, :]
            ).astype(jnp.bfloat16)
        writes.append(
            pltpu.make_async_copy(out_tiles.at[step], out_ref.at[own, :], out_sem.at[step])
        )
        writes[-1].start()
    for write in writes:
        write.wait()


def last_product(keep, total, a_last, a_groups, b_blocks, b_place, mesh_sizes):
    arrays, distances = zip(*a_groups, strict=True)
    a_rows, columns = total.shape
    inner = a_last.shape[1] * (mesh_sizes[0] + 1)
    rows = 2 * TILE
    steps = a_rows // rows
    return pl.pallas_call(
        functools.partial(last_kernel, distances, b_place, mesh_sizes),
        out_shape=jax.ShapeDtypeStruct((a_rows, columns), jnp.bfloat16),
        in_specs=[VMEM] * (3 + len(arrays) + len(b_blocks)),
        out_specs=ANY,
        scratch_shapes=[
            pltpu.VMEM((a_rows, inner), jnp.bfloat16),
            pltpu.VMEM((steps, rows, columns), jnp.bfloat16),
            pltpu.SemaphoreType.DMA((steps,)),
        ],
        compiler_params=LIMITS,
        cost_estimate=cost(2 * a_rows * inner * columns, 6 * total.size),
    )(*(near(array) for array in (keep, total, a_last, *arrays, *b_blocks)))


def swapped(block, axis, distance):
    return lax.ppermute(block, axis, [(i, i ^ distance) for i in range(lax.axis_size(axis))])


def crossed(block, even, odd):
    cols = lax.axis_size("col")
    pairs = [
        (r * cols + c, (r ^ (odd if c % 2 else even)) * cols + c)
        for r in range(lax.axis_size("row"))
        for c in range(cols)
    ]
    return lax.ppermute(block, ("row", "col"), pairs)


def gathered_b(b_eff):
    rows = lax.axis_size("row")
    if rows != 4:
        return [b_eff] + [swapped(b_eff, "row", d) for d in range(1, rows)], lambda distance: distance
    first = crossed(b_eff, 1, 2)
    second = crossed(b_eff, 2, 1)
    last = crossed(first, 2, 1)

    def place(distance):
        odd = lax.axis_index("col") & 1
        return jnp.where((distance == 0) | (distance == 3), distance, distance ^ (3 * odd))

    return [b_eff, first, second, last], place


def beside_kernel(*refs):
    *block_refs, out_ref = refs
    width = block_refs[0].shape[1]
    for i, block_ref in enumerate(block_refs):
        out_ref[:, i * width : (i + 1) * width] = block_ref[...]


def beside(blocks):
    rows, width = blocks[0].shape
    return pl.pallas_call(
        beside_kernel,
        out_shape=pltpu.VMEM((rows, width * len(blocks)), blocks[0].dtype),
        in_specs=[VMEM] * len(blocks),
        out_specs=VMEM,
        compiler_params=LIMITS,
        cost_estimate=cost(0, 4 * rows * width * len(blocks)),
    )(*(near(block) for block in blocks))


def started_early(block):
    return pl.pallas_call(
        lambda block_ref, same_ref: None,
        out_shape=pltpu.VMEM(block.shape, block.dtype),
        in_specs=[VMEM],
        out_specs=VMEM,
        input_output_aliases={0: 0},
        cost_estimate=cost(460_000_000, 0),
    )(near(block))


def gathered_a(a_eff):
    cols = lax.axis_size("col")
    blocks = {0: a_eff} | {d: swapped(a_eff, "col", d) for d in range(2, cols, 2)}
    if cols == 8:
        blocks[6] = started_early(blocks[6])
        groups = ((0, 4), (2, 6))
    else:
        groups = (tuple(blocks)[: cols // 4], tuple(blocks)[cols // 4 :])
    owns = [(beside([blocks[d] for d in group]), group) for group in groups]
    partners = [(swapped(own, "col", 1), tuple(d ^ 1 for d in group)) for own, group in owns]
    return owns, partners


def per_device(row_ids, a_tiles, a_mask, b_tiles, b_mask, c_keep):
    sizes = (lax.axis_size("row"), lax.axis_size("col"))
    assert sizes[1] == 2 * sizes[0] and b_tiles.shape[0] == 2 * a_tiles.shape[1]
    a_eff, b_eff = masked(a_tiles, a_mask, b_tiles, b_mask)
    b_blocks, b_place = gathered_b(b_eff)
    owns, partners = gathered_a(a_eff)
    total, a_last, keep = early_product(row_ids, c_keep, owns, b_blocks[:-1], b_place, sizes)
    return last_product(keep, total, a_last, partners, b_blocks, b_place, sizes)


def solution(mesh):
    placed = (
        P("row"),
        P("row", "col"),
        P("row", "col"),
        P("row", "col"),
        P("row", "col"),
        P(None, "col"),
    )
    return jax.shard_map(
        per_device, mesh=mesh, in_specs=placed, out_specs=P("row", "col"), check_vma=False
    )
```

```python
import functools

import jax
import jax.numpy as jnp
from jax import lax
from jax.experimental import pallas as pl
from jax.experimental.pallas import tpu as pltpu
from jax.sharding import PartitionSpec as P

TILE = 64
ANY = pl.BlockSpec(memory_space=pl.ANY)
VMEM = pl.BlockSpec(memory_space=pltpu.VMEM)
SMEM = pl.BlockSpec(memory_space=pltpu.SMEM)
LIMITS = pltpu.CompilerParams(vmem_limit_bytes=24 * 1024 * 1024)


def near(array):
    return pltpu.with_memory_space_constraint(array, pltpu.VMEM)


def cost(flops, bytes_accessed):
    return pl.CostEstimate(flops=flops, bytes_accessed=bytes_accessed, transcendentals=0)


def keep_present(mask_at, tiles_ref, out_ref):
    lane = lax.broadcasted_iota(jnp.int32, (TILE, 2 * TILE), 1)
    for i in range(tiles_ref.shape[0] // TILE):
        for j in range(0, tiles_ref.shape[1] // TILE, 2):
            place = (pl.ds(i * TILE, TILE), pl.ds(j * TILE, 2 * TILE))
            present = jnp.where(lane < TILE, mask_at(i, j), mask_at(i, j + 1)) != 0
            tiles = tiles_ref[place]
            out_ref[place] = jnp.where(present, tiles, jnp.zeros_like(tiles))


def mask_kernel(a_mask_ref, b_mask_ref, a_ref, b_ref, a_out_ref, b_out_ref):
    keep_present(lambda i, j: b_mask_ref[i, j], b_ref, b_out_ref)
    keep_present(lambda i, j: a_mask_ref[j, i], a_ref, a_out_ref)


def masked(a_tiles, a_mask, b_tiles, b_mask):
    size = a_tiles.size + b_tiles.size
    return pl.pallas_call(
        mask_kernel,
        out_shape=(
            pltpu.VMEM(a_tiles.shape, a_tiles.dtype),
            pltpu.VMEM(b_tiles.shape, b_tiles.dtype),
        ),
        in_specs=[SMEM, SMEM, VMEM, VMEM],
        out_specs=(VMEM, VMEM),
        cost_estimate=cost(size, 4 * size),
    )(a_mask.T, b_mask, a_tiles, b_tiles)


def spread(mask):
    shape = (mask.shape[1], mask.shape[1] * TILE)
    owner = lax.broadcasted_iota(jnp.int32, shape, 1) // TILE
    ones = (owner == lax.broadcasted_iota(jnp.int32, shape, 0)).astype(jnp.float32)
    return jnp.dot(mask, ones, preferred_element_type=jnp.float32)


def met_by(distance, b_place, mesh_sizes):
    row_count, col_count = mesh_sizes
    ratio = col_count // row_count
    me_row, me_col = lax.axis_index("row"), lax.axis_index("col")
    shift = (me_col ^ distance) - me_col
    stored = lax.rem(shift + ratio * me_row + ratio - 1 + 2 * col_count, col_count)
    return b_place((stored // ratio) ^ me_row)


def early_kernel(own_distances, partner_distances, b_place, mesh_sizes, row_ids_ref, c_keep_ref, *refs):
    row_count = mesh_sizes[0]
    early = row_count - 1
    own_refs, refs = refs[: len(own_distances)], refs[len(own_distances) :]
    partner_ref, *refs = refs
    b_refs, (total_ref, tail_ref, keep_ref, firsts_ref, panels) = refs[:early], refs[early:]
    width = b_refs[0].shape[0] // 2

    def put(block, distance, side):
        place = met_by(distance, b_place, mesh_sizes)
        slot = jnp.where(place == early, 2 * early + side, side * early + place)
        panels[:, pl.ds(pl.multiple_of(slot * width, width), width)] = block

    for array_ref, distances in zip(own_refs, own_distances, strict=True):
        for i, distance in enumerate(distances):
            put(array_ref[:, i * width : (i + 1) * width], distance, 0)
    panels[:, early * width : 2 * early * width] = jnp.zeros(
        (panels.shape[0], early * width), panels.dtype
    )
    panels[:, (2 * early + 1) * width :] = jnp.zeros((panels.shape[0], width), panels.dtype)
    for i, distance in enumerate(partner_distances):
        put(partner_ref[:, i * width : (i + 1) * width], distance, 1)
    tail_ref[...] = panels[:, 2 * early * width :]
    for place, b_ref in enumerate(b_refs):
        firsts_ref[place * width : (place + 1) * width, :] = b_ref[:width, :]
    blocks = jnp.concatenate(
        [b_ref[width:, :] for b_ref in b_refs] + [b_ref[:width, :] for b_ref in b_refs], axis=0
    )
    for start in range(0, total_ref.shape[0], 2 * TILE):
        rows = pl.ds(start, 2 * TILE)
        total_ref[rows, :] = jnp.dot(
            panels[rows, : 2 * early * width], blocks, preferred_element_type=jnp.float32
        )
    ids = row_ids_ref[...]
    which = lax.broadcasted_iota(jnp.int32, (ids.shape[0], c_keep_ref.shape[1]), 1)
    keep_ref[...] = spread(
        lax.dot_general(
            (ids == which).astype(jnp.float32),
            c_keep_ref[...].astype(jnp.float32),
            (((1,), (1,)), ((), ())),
            preferred_element_type=jnp.float32,
        )
    )


def early_product(row_ids, c_keep, owns, partner, b_blocks, b_place, mesh_sizes):
    arrays, distances = zip(*owns, strict=True)
    partner_array, partner_distances = partner
    a_rows = arrays[0].shape[0]
    depth, columns = b_blocks[0].shape
    width, early = depth // 2, len(b_blocks)
    return pl.pallas_call(
        functools.partial(early_kernel, distances, partner_distances, b_place, mesh_sizes),
        out_shape=(
            pltpu.VMEM((a_rows, columns), jnp.float32),
            pltpu.VMEM((a_rows, depth), jnp.bfloat16),
            pltpu.VMEM((row_ids.shape[0], columns), jnp.float32),
            pltpu.VMEM(((early + 1) * width, columns), jnp.bfloat16),
        ),
        in_specs=[VMEM] * (3 + len(arrays) + len(b_blocks)),
        out_specs=(VMEM,) * 4,
        scratch_shapes=[pltpu.VMEM((a_rows, (2 * early + 2) * width), jnp.bfloat16)],
        compiler_params=LIMITS,
        cost_estimate=cost(2 * a_rows * width * early * columns, 4 * a_rows * columns),
    )(
        near(row_ids[:, None]),
        near(c_keep.T),
        *(near(block) for block in (*arrays, partner_array, *b_blocks)),
    )


def last_kernel(distances, b_place, mesh_sizes, keep_ref, total_ref, tail_ref, a_ref, b_ref, firsts_in_ref, out_ref, firsts_ref, out_tiles, out_sem):
    width = b_ref.shape[0] // 2
    firsts_ref[(mesh_sizes[0] - 1) * width :, :] = b_ref[:width, :]
    panels = []
    for distance in distances:
        place = met_by(distance, b_place, mesh_sizes)
        panels.append(firsts_ref[pl.ds(pl.multiple_of(place * width, width), width), :])
    blocks = jnp.concatenate(panels + [b_ref[width:, :], b_ref[:width, :]], axis=0)
    rows = out_tiles.shape[1]
    writes = []
    for step in range(out_tiles.shape[0]):
        own = pl.ds(step * rows, rows)
        total = total_ref[own, :] + jnp.dot(
            jnp.concatenate([a_ref[own, :], tail_ref[own, :]], axis=1),
            blocks,
            preferred_element_type=jnp.float32,
        )
        for i in range(rows // TILE):
            slot = step * rows // TILE + i
            out_tiles[step, pl.ds(i * TILE, TILE), :] = (
                total[i * TILE : (i + 1) * TILE] * keep_ref[slot : slot + 1, :]
            ).astype(jnp.bfloat16)
        writes.append(
            pltpu.make_async_copy(out_tiles.at[step], out_ref.at[own, :], out_sem.at[step])
        )
        writes[-1].start()
    for write in writes:
        write.wait()


def last_product(keep, total, tail, firsts, partner, b_last, b_place, mesh_sizes):
    array, distances = partner
    a_rows, columns = total.shape
    inner = array.shape[1] + tail.shape[1]
    rows = 2 * TILE
    steps = a_rows // rows
    return pl.pallas_call(
        functools.partial(last_kernel, distances, b_place, mesh_sizes),
        out_shape=(
            jax.ShapeDtypeStruct((a_rows, columns), jnp.bfloat16),
            pltpu.VMEM(firsts.shape, firsts.dtype),
        ),
        in_specs=[VMEM] * 6,
        out_specs=(ANY, VMEM),
        input_output_aliases={5: 1},
        scratch_shapes=[
            pltpu.VMEM((steps, rows, columns), jnp.bfloat16),
            pltpu.SemaphoreType.DMA((steps,)),
        ],
        compiler_params=LIMITS,
        cost_estimate=cost(2 * a_rows * inner * columns, 6 * total.size),
    )(*(near(operand) for operand in (keep, total, tail, array, b_last, firsts)))[0]


def swapped(block, axis, distance):
    return lax.ppermute(block, axis, [(i, i ^ distance) for i in range(lax.axis_size(axis))])


def crossed(block, even, odd):
    cols = lax.axis_size("col")
    pairs = [
        (r * cols + c, (r ^ (odd if c % 2 else even)) * cols + c)
        for r in range(lax.axis_size("row"))
        for c in range(cols)
    ]
    return lax.ppermute(block, ("row", "col"), pairs)


def gathered_b(b_eff):
    rows = lax.axis_size("row")
    if rows != 4:
        return [b_eff] + [swapped(b_eff, "row", d) for d in range(1, rows)], lambda distance: distance
    first = crossed(b_eff, 1, 2)
    second = crossed(b_eff, 2, 1)
    last = crossed(first, 2, 1)

    def place(distance):
        odd = lax.axis_index("col") & 1
        return jnp.where((distance == 0) | (distance == 3), distance, distance ^ (3 * odd))

    return [b_eff, first, second, last], place


def beside_kernel(*refs):
    *block_refs, out_ref = refs
    width = block_refs[0].shape[1]
    for i, block_ref in enumerate(block_refs):
        out_ref[:, i * width : (i + 1) * width] = block_ref[...]


def beside(blocks):
    rows, width = blocks[0].shape
    return pl.pallas_call(
        beside_kernel,
        out_shape=pltpu.VMEM((rows, width * len(blocks)), blocks[0].dtype),
        in_specs=[VMEM] * len(blocks),
        out_specs=VMEM,
        compiler_params=LIMITS,
        cost_estimate=cost(0, 4 * rows * width * len(blocks)),
    )(*(near(block) for block in blocks))


def started_early(block):
    return pl.pallas_call(
        lambda block_ref, same_ref: None,
        out_shape=pltpu.VMEM(block.shape, block.dtype),
        in_specs=[VMEM],
        out_specs=VMEM,
        input_output_aliases={0: 0},
        cost_estimate=cost(460_000_000, 0),
    )(near(block))


def gathered_a(a_eff):
    cols = lax.axis_size("col")
    blocks = {0: a_eff} | {d: swapped(a_eff, "col", d) for d in range(2, cols, 2)}
    if cols == 8:
        blocks[6] = started_early(blocks[6])
        groups = ((0, 4), (2, 6))
    else:
        groups = (tuple(blocks)[: cols // 4], tuple(blocks)[cols // 4 :])
    owns = [(beside([blocks[d] for d in group]), group) for group in groups]
    partners = [(swapped(own, "col", 1), tuple(d ^ 1 for d in group)) for own, group in owns]
    return owns, partners


def per_device(row_ids, a_tiles, a_mask, b_tiles, b_mask, c_keep):
    sizes = (lax.axis_size("row"), lax.axis_size("col"))
    assert sizes[1] == 2 * sizes[0] and b_tiles.shape[0] == 2 * a_tiles.shape[1]
    a_eff, b_eff = masked(a_tiles, a_mask, b_tiles, b_mask)
    b_blocks, b_place = gathered_b(b_eff)
    owns, partners = gathered_a(a_eff)
    total, tail, keep, firsts = early_product(
        row_ids, c_keep, owns, partners[0], b_blocks[:-1], b_place, sizes
    )
    return last_product(keep, total, tail, firsts, partners[1], b_blocks[-1], b_place, sizes)


def solution(mesh):
    placed = (
        P("row"),
        P("row", "col"),
        P("row", "col"),
        P("row", "col"),
        P("row", "col"),
        P(None, "col"),
    )
    return jax.shard_map(
        per_device, mesh=mesh, in_specs=placed, out_specs=P("row", "col"), check_vma=False
    )
```

```python
import functools

import jax
import jax.numpy as jnp
from jax import lax
from jax.experimental import pallas as pl
from jax.experimental.pallas import tpu as pltpu
from jax.sharding import PartitionSpec as P

TILE = 64
ANY = pl.BlockSpec(memory_space=pl.ANY)
VMEM = pl.BlockSpec(memory_space=pltpu.VMEM)
SMEM = pl.BlockSpec(memory_space=pltpu.SMEM)
LIMITS = pltpu.CompilerParams(vmem_limit_bytes=24 * 1024 * 1024)


def near(array):
    return pltpu.with_memory_space_constraint(array, pltpu.VMEM)


def cost(flops, bytes_accessed):
    return pl.CostEstimate(flops=flops, bytes_accessed=bytes_accessed, transcendentals=0)


def keep_present(mask_at, tiles_ref, out_ref):
    lane = lax.broadcasted_iota(jnp.int32, (TILE, 2 * TILE), 1)
    for i in range(tiles_ref.shape[0] // TILE):
        for j in range(0, tiles_ref.shape[1] // TILE, 2):
            place = (pl.ds(i * TILE, TILE), pl.ds(j * TILE, 2 * TILE))
            present = jnp.where(lane < TILE, mask_at(i, j), mask_at(i, j + 1)) != 0
            tiles = tiles_ref[place]
            out_ref[place] = jnp.where(present, tiles, jnp.zeros_like(tiles))


def mask_kernel(a_mask_ref, b_mask_ref, a_ref, b_ref, a_out_ref, b_out_ref):
    keep_present(lambda i, j: b_mask_ref[i, j], b_ref, b_out_ref)
    keep_present(lambda i, j: a_mask_ref[j, i], a_ref, a_out_ref)


def masked(a_tiles, a_mask, b_tiles, b_mask):
    size = a_tiles.size + b_tiles.size
    return pl.pallas_call(
        mask_kernel,
        out_shape=(
            pltpu.VMEM(a_tiles.shape, a_tiles.dtype),
            pltpu.VMEM(b_tiles.shape, b_tiles.dtype),
        ),
        in_specs=[SMEM, SMEM, VMEM, VMEM],
        out_specs=(VMEM, VMEM),
        cost_estimate=cost(size, 4 * size),
    )(a_mask.T, b_mask, a_tiles, b_tiles)


def spread(mask):
    shape = (mask.shape[1], mask.shape[1] * TILE)
    owner = lax.broadcasted_iota(jnp.int32, shape, 1) // TILE
    ones = (owner == lax.broadcasted_iota(jnp.int32, shape, 0)).astype(jnp.float32)
    return jnp.dot(mask, ones, preferred_element_type=jnp.float32)


def met_by(distance, b_place, mesh_sizes):
    row_count, col_count = mesh_sizes
    ratio = col_count // row_count
    me_row, me_col = lax.axis_index("row"), lax.axis_index("col")
    shift = (me_col ^ distance) - me_col
    stored = lax.rem(shift + ratio * me_row + ratio - 1 + 2 * col_count, col_count)
    return b_place((stored // ratio) ^ me_row)


def early_kernel(own_distances, partner_distances, b_place, mesh_sizes, row_ids_ref, c_keep_ref, *refs):
    row_count = mesh_sizes[0]
    early = row_count - 1
    own_refs, refs = refs[: len(own_distances)], refs[len(own_distances) :]
    partner_ref, *refs = refs
    b_refs, (total_ref, tail_ref, keep_ref, firsts_ref, panels) = refs[:early], refs[early:]
    width = b_refs[0].shape[0] // 2

    def put(block, distance, side):
        place = met_by(distance, b_place, mesh_sizes)
        slot = jnp.where(place == early, 2 * early + 1 - side, side * early + place)
        panels[:, pl.ds(pl.multiple_of(slot * width, width), width)] = block

    for array_ref, distances in zip(own_refs, own_distances, strict=True):
        for i, distance in enumerate(distances):
            put(array_ref[:, i * width : (i + 1) * width], distance, 0)
    panels[:, early * width : (2 * early + 1) * width] = jnp.zeros(
        (panels.shape[0], (early + 1) * width), panels.dtype
    )
    for i, distance in enumerate(partner_distances):
        put(partner_ref[:, i * width : (i + 1) * width], distance, 1)
    tail_ref[...] = panels[:, 2 * early * width :]
    for place, b_ref in enumerate(b_refs):
        firsts_ref[place * width : (place + 1) * width, :] = b_ref[:width, :]
    blocks = jnp.concatenate(
        [b_ref[width:, :] for b_ref in b_refs] + [b_ref[:width, :] for b_ref in b_refs], axis=0
    )
    for start in range(0, total_ref.shape[0], 2 * TILE):
        rows = pl.ds(start, 2 * TILE)
        total_ref[rows, :] = jnp.dot(
            panels[rows, : 2 * early * width], blocks, preferred_element_type=jnp.float32
        )
    ids = row_ids_ref[...]
    which = lax.broadcasted_iota(jnp.int32, (c_keep_ref.shape[1], ids.shape[1]), 0)
    keep_ref[...] = spread(
        lax.dot_general(
            (ids == which).astype(jnp.float32),
            c_keep_ref[...].astype(jnp.float32),
            (((0,), (1,)), ((), ())),
            preferred_element_type=jnp.float32,
        )
    )


def early_product(row_ids, c_keep, owns, partner, b_blocks, b_place, mesh_sizes):
    arrays, distances = zip(*owns, strict=True)
    partner_array, partner_distances = partner
    a_rows = arrays[0].shape[0]
    depth, columns = b_blocks[0].shape
    width, early = depth // 2, len(b_blocks)
    return pl.pallas_call(
        functools.partial(early_kernel, distances, partner_distances, b_place, mesh_sizes),
        out_shape=(
            pltpu.VMEM((a_rows, columns), jnp.float32),
            pltpu.VMEM((a_rows, depth), jnp.bfloat16),
            pltpu.VMEM((row_ids.shape[0], columns), jnp.float32),
            pltpu.VMEM(((early + 1) * width, columns), jnp.bfloat16),
        ),
        in_specs=[VMEM] * (3 + len(arrays) + len(b_blocks)),
        out_specs=(VMEM,) * 4,
        scratch_shapes=[pltpu.VMEM((a_rows, (2 * early + 2) * width), jnp.bfloat16)],
        compiler_params=LIMITS,
        cost_estimate=cost(2 * a_rows * width * early * columns, 4 * a_rows * columns),
    )(
        near(row_ids[None, :]),
        near(c_keep.T),
        *(near(block) for block in (*arrays, partner_array, *b_blocks)),
    )


def last_kernel(distances, b_place, mesh_sizes, keep_ref, total_ref, tail_ref, a_ref, b_ref, firsts_in_ref, out_ref, firsts_ref, out_tiles, out_sem):
    width = b_ref.shape[0] // 2
    firsts_ref[(mesh_sizes[0] - 1) * width :, :] = b_ref[:width, :]
    panels = []
    for distance in distances:
        place = met_by(distance, b_place, mesh_sizes)
        panels.append(firsts_ref[pl.ds(pl.multiple_of(place * width, width), width), :])
    blocks = jnp.concatenate(panels, axis=0)
    rows = out_tiles.shape[1]
    writes = []
    for step in range(out_tiles.shape[0]):
        own = pl.ds(step * rows, rows)
        total = total_ref[own, :] + jnp.dot(
            tail_ref[own, :], b_ref[...], preferred_element_type=jnp.float32
        )
        total = total + jnp.dot(a_ref[own, :], blocks, preferred_element_type=jnp.float32)
        for i in range(rows // TILE):
            slot = step * rows // TILE + i
            out_tiles[step, pl.ds(i * TILE, TILE), :] = (
                total[i * TILE : (i + 1) * TILE] * keep_ref[slot : slot + 1, :]
            ).astype(jnp.bfloat16)
        writes.append(
            pltpu.make_async_copy(out_tiles.at[step], out_ref.at[own, :], out_sem.at[step])
        )
        writes[-1].start()
    for write in writes:
        write.wait()


def last_product(keep, total, tail, firsts, partner, b_last, b_place, mesh_sizes):
    array, distances = partner
    a_rows, columns = total.shape
    inner = array.shape[1] + tail.shape[1]
    rows = 2 * TILE
    steps = a_rows // rows
    return pl.pallas_call(
        functools.partial(last_kernel, distances, b_place, mesh_sizes),
        out_shape=(
            jax.ShapeDtypeStruct((a_rows, columns), jnp.bfloat16),
            pltpu.VMEM(firsts.shape, firsts.dtype),
        ),
        in_specs=[VMEM] * 6,
        out_specs=(ANY, VMEM),
        input_output_aliases={5: 1},
        scratch_shapes=[
            pltpu.VMEM((steps, rows, columns), jnp.bfloat16),
            pltpu.SemaphoreType.DMA((steps,)),
        ],
        compiler_params=LIMITS,
        cost_estimate=cost(2 * a_rows * inner * columns, 6 * total.size),
    )(*(near(operand) for operand in (keep, total, tail, array, b_last, firsts)))[0]


def swapped(block, axis, distance):
    return lax.ppermute(block, axis, [(i, i ^ distance) for i in range(lax.axis_size(axis))])


def crossed(block, even, odd):
    cols = lax.axis_size("col")
    pairs = [
        (r * cols + c, (r ^ (odd if c % 2 else even)) * cols + c)
        for r in range(lax.axis_size("row"))
        for c in range(cols)
    ]
    return lax.ppermute(block, ("row", "col"), pairs)


def gathered_b(b_eff):
    rows = lax.axis_size("row")
    if rows != 4:
        return [b_eff] + [swapped(b_eff, "row", d) for d in range(1, rows)], lambda distance: distance
    first = crossed(b_eff, 1, 2)
    second = crossed(b_eff, 2, 1)
    last = crossed(first, 2, 1)

    def place(distance):
        odd = lax.axis_index("col") & 1
        return jnp.where((distance == 0) | (distance == 3), distance, distance ^ (3 * odd))

    return [b_eff, first, second, last], place


def beside_kernel(*refs):
    *block_refs, out_ref = refs
    width = block_refs[0].shape[1]
    for i, block_ref in enumerate(block_refs):
        out_ref[:, i * width : (i + 1) * width] = block_ref[...]


def beside(blocks):
    rows, width = blocks[0].shape
    return pl.pallas_call(
        beside_kernel,
        out_shape=pltpu.VMEM((rows, width * len(blocks)), blocks[0].dtype),
        in_specs=[VMEM] * len(blocks),
        out_specs=VMEM,
        compiler_params=LIMITS,
        cost_estimate=cost(0, 4 * rows * width * len(blocks)),
    )(*(near(block) for block in blocks))


def started_early(block):
    return pl.pallas_call(
        lambda block_ref, same_ref: None,
        out_shape=pltpu.VMEM(block.shape, block.dtype),
        in_specs=[VMEM],
        out_specs=VMEM,
        input_output_aliases={0: 0},
        cost_estimate=cost(460_000_000, 0),
    )(near(block))


def gathered_a(a_eff):
    cols = lax.axis_size("col")
    blocks = {0: a_eff} | {d: swapped(a_eff, "col", d) for d in range(2, cols, 2)}
    if cols == 8:
        blocks[6] = started_early(blocks[6])
        groups = ((0, 4), (2, 6))
    else:
        groups = (tuple(blocks)[: cols // 4], tuple(blocks)[cols // 4 :])
    owns = [(beside([blocks[d] for d in group]), group) for group in groups]
    partners = [(swapped(own, "col", 1), tuple(d ^ 1 for d in group)) for own, group in owns]
    return owns, partners


def per_device(row_ids, a_tiles, a_mask, b_tiles, b_mask, c_keep):
    sizes = (lax.axis_size("row"), lax.axis_size("col"))
    assert sizes[1] == 2 * sizes[0] and b_tiles.shape[0] == 2 * a_tiles.shape[1]
    a_eff, b_eff = masked(a_tiles, a_mask, b_tiles, b_mask)
    b_blocks, b_place = gathered_b(b_eff)
    owns, partners = gathered_a(a_eff)
    total, tail, keep, firsts = early_product(
        row_ids, c_keep, owns, partners[0], b_blocks[:-1], b_place, sizes
    )
    return last_product(keep, total, tail, firsts, partners[1], b_blocks[-1], b_place, sizes)


def solution(mesh):
    placed = (
        P("row"),
        P("row", "col"),
        P("row", "col"),
        P("row", "col"),
        P("row", "col"),
        P(None, "col"),
    )
    return jax.shard_map(
        per_device, mesh=mesh, in_specs=placed, out_specs=P("row", "col"), check_vma=False
    )
```

```python
import functools

import jax
import jax.numpy as jnp
from jax import lax
from jax.experimental import pallas as pl
from jax.experimental.pallas import tpu as pltpu
from jax.sharding import PartitionSpec as P

TILE = 64
ANY = pl.BlockSpec(memory_space=pl.ANY)
VMEM = pl.BlockSpec(memory_space=pltpu.VMEM)
SMEM = pl.BlockSpec(memory_space=pltpu.SMEM)
LIMITS = pltpu.CompilerParams(vmem_limit_bytes=24 * 1024 * 1024)


def near(array):
    return pltpu.with_memory_space_constraint(array, pltpu.VMEM)


def cost(flops, bytes_accessed):
    return pl.CostEstimate(flops=flops, bytes_accessed=bytes_accessed, transcendentals=0)


def keep_present(mask_at, tiles_ref, out_ref):
    lane = lax.broadcasted_iota(jnp.int32, (TILE, 2 * TILE), 1)
    for i in range(tiles_ref.shape[0] // TILE):
        for j in range(0, tiles_ref.shape[1] // TILE, 2):
            place = (pl.ds(i * TILE, TILE), pl.ds(j * TILE, 2 * TILE))
            present = jnp.where(lane < TILE, mask_at(i, j), mask_at(i, j + 1)) != 0
            tiles = tiles_ref[place]
            out_ref[place] = jnp.where(present, tiles, jnp.zeros_like(tiles))


def mask_kernel(a_mask_ref, b_mask_ref, a_ref, b_ref, a_out_ref, b_out_ref):
    keep_present(lambda i, j: b_mask_ref[i, j], b_ref, b_out_ref)
    keep_present(lambda i, j: a_mask_ref[j, i], a_ref, a_out_ref)


def masked(a_tiles, a_mask, b_tiles, b_mask):
    size = a_tiles.size + b_tiles.size
    return pl.pallas_call(
        mask_kernel,
        out_shape=(
            pltpu.VMEM(a_tiles.shape, a_tiles.dtype),
            pltpu.VMEM(b_tiles.shape, b_tiles.dtype),
        ),
        in_specs=[SMEM, SMEM, VMEM, VMEM],
        out_specs=(VMEM, VMEM),
        cost_estimate=cost(size, 4 * size),
    )(a_mask.T, b_mask, a_tiles, b_tiles)


def spread(mask):
    shape = (mask.shape[1], mask.shape[1] * TILE)
    owner = lax.broadcasted_iota(jnp.int32, shape, 1) // TILE
    ones = (owner == lax.broadcasted_iota(jnp.int32, shape, 0)).astype(jnp.float32)
    return jnp.dot(mask, ones, preferred_element_type=jnp.float32)


def met_by(distance, b_place, mesh_sizes):
    row_count, col_count = mesh_sizes
    ratio = col_count // row_count
    me_row, me_col = lax.axis_index("row"), lax.axis_index("col")
    shift = (me_col ^ distance) - me_col
    stored = lax.rem(shift + ratio * me_row + ratio - 1 + 2 * col_count, col_count)
    return b_place((stored // ratio) ^ me_row)


def early_kernel(own_distances, partner_distances, b_place, mesh_sizes, row_ids_ref, c_keep_ref, *refs):
    row_count = mesh_sizes[0]
    early = row_count - 1
    own_refs, refs = refs[: len(own_distances)], refs[len(own_distances) :]
    partner_ref, *refs = refs
    b_refs, (total_ref, tail_ref, keep_ref, firsts_ref, panels) = refs[:early], refs[early:]
    width = b_refs[0].shape[0] // 2

    def put(block, distance, side):
        place = met_by(distance, b_place, mesh_sizes)
        slot = jnp.where(place == early, 2 * early + side, side * early + place)
        panels[:, pl.ds(pl.multiple_of(slot * width, width), width)] = block

    for array_ref, distances in zip(own_refs, own_distances, strict=True):
        for i, distance in enumerate(distances):
            put(array_ref[:, i * width : (i + 1) * width], distance, 0)
    panels[:, early * width : 2 * early * width] = jnp.zeros(
        (panels.shape[0], early * width), panels.dtype
    )
    panels[:, (2 * early + 1) * width :] = jnp.zeros((panels.shape[0], width), panels.dtype)
    for i, distance in enumerate(partner_distances):
        put(partner_ref[:, i * width : (i + 1) * width], distance, 1)
    tail_ref[...] = panels[:, 2 * early * width :]
    for place, b_ref in enumerate(b_refs):
        firsts_ref[place * width : (place + 1) * width, :] = b_ref[:width, :]
    blocks = jnp.concatenate(
        [b_ref[width:, :] for b_ref in b_refs] + [b_ref[:width, :] for b_ref in b_refs], axis=0
    )
    for start in range(0, total_ref.shape[0], 2 * TILE):
        rows = pl.ds(start, 2 * TILE)
        total_ref[rows, :] = jnp.dot(
            panels[rows, : 2 * early * width], blocks, preferred_element_type=jnp.float32
        )
    ids = row_ids_ref[...]
    which = lax.broadcasted_iota(jnp.int32, (ids.shape[0], c_keep_ref.shape[1]), 1)
    keep_ref[...] = spread(
        lax.dot_general(
            (ids == which).astype(jnp.float32),
            c_keep_ref[...].astype(jnp.float32),
            (((1,), (1,)), ((), ())),
            preferred_element_type=jnp.float32,
        )
    )


def early_product(row_ids, c_keep, owns, partner, b_blocks, b_place, mesh_sizes):
    arrays, distances = zip(*owns, strict=True)
    partner_array, partner_distances = partner
    a_rows = arrays[0].shape[0]
    depth, columns = b_blocks[0].shape
    width, early = depth // 2, len(b_blocks)
    return pl.pallas_call(
        functools.partial(early_kernel, distances, partner_distances, b_place, mesh_sizes),
        out_shape=(
            pltpu.VMEM((a_rows, columns), jnp.float32),
            pltpu.VMEM((a_rows, depth), jnp.bfloat16),
            pltpu.VMEM((row_ids.shape[0], columns), jnp.float32),
            pltpu.VMEM(((early + 1) * width, columns), jnp.bfloat16),
        ),
        in_specs=[VMEM] * (3 + len(arrays) + len(b_blocks)),
        out_specs=(VMEM,) * 4,
        scratch_shapes=[pltpu.VMEM((a_rows, (2 * early + 2) * width), jnp.bfloat16)],
        compiler_params=LIMITS,
        cost_estimate=cost(2 * a_rows * width * early * columns, 4 * a_rows * columns),
    )(
        near(row_ids[:, None]),
        near(c_keep.T),
        *(near(block) for block in (*arrays, partner_array, *b_blocks)),
    )


def last_kernel(distances, b_place, mesh_sizes, keep_ref, total_ref, tail_ref, a_ref, b_ref, firsts_in_ref, out_ref, firsts_ref, out_tiles, out_sem):
    width = b_ref.shape[0] // 2
    firsts_ref[(mesh_sizes[0] - 1) * width :, :] = b_ref[:width, :]
    panels = []
    for distance in distances:
        place = met_by(distance, b_place, mesh_sizes)
        panels.append(firsts_ref[pl.ds(pl.multiple_of(place * width, width), width), :])
    blocks = jnp.concatenate(panels + [b_ref[width:, :], b_ref[:width, :]], axis=0)
    rows = out_tiles.shape[1]
    writes = []
    for step in range(out_tiles.shape[0]):
        own = pl.ds(step * rows, rows)
        total = total_ref[own, :] + jnp.dot(
            jnp.concatenate([a_ref[own, :], tail_ref[own, :]], axis=1),
            blocks,
            preferred_element_type=jnp.float32,
        )
        for i in range(rows // TILE):
            slot = step * rows // TILE + i
            out_tiles[step, pl.ds(i * TILE, TILE), :] = (
                total[i * TILE : (i + 1) * TILE] * keep_ref[slot : slot + 1, :]
            ).astype(jnp.bfloat16)
            writes.append(
                pltpu.make_async_copy(
                    out_tiles.at[step, pl.ds(i * TILE, TILE)],
                    out_ref.at[pl.ds(slot * TILE, TILE), :],
                    out_sem.at[slot],
                )
            )
            writes[-1].start()
    for write in writes:
        write.wait()


def last_product(keep, total, tail, firsts, partner, b_last, b_place, mesh_sizes):
    array, distances = partner
    a_rows, columns = total.shape
    inner = array.shape[1] + tail.shape[1]
    rows = 2 * TILE
    steps = a_rows // rows
    return pl.pallas_call(
        functools.partial(last_kernel, distances, b_place, mesh_sizes),
        out_shape=(
            jax.ShapeDtypeStruct((a_rows, columns), jnp.bfloat16),
            pltpu.VMEM(firsts.shape, firsts.dtype),
        ),
        in_specs=[VMEM] * 6,
        out_specs=(ANY, VMEM),
        input_output_aliases={5: 1},
        scratch_shapes=[
            pltpu.VMEM((steps, rows, columns), jnp.bfloat16),
            pltpu.SemaphoreType.DMA((a_rows // TILE,)),
        ],
        compiler_params=LIMITS,
        cost_estimate=cost(2 * a_rows * inner * columns, 6 * total.size),
    )(*(near(operand) for operand in (keep, total, tail, array, b_last, firsts)))[0]


def swapped(block, axis, distance):
    return lax.ppermute(block, axis, [(i, i ^ distance) for i in range(lax.axis_size(axis))])


def crossed(block, even, odd):
    cols = lax.axis_size("col")
    pairs = [
        (r * cols + c, (r ^ (odd if c % 2 else even)) * cols + c)
        for r in range(lax.axis_size("row"))
        for c in range(cols)
    ]
    return lax.ppermute(block, ("row", "col"), pairs)


def gathered_b(b_eff):
    rows = lax.axis_size("row")
    if rows != 4:
        return [b_eff] + [swapped(b_eff, "row", d) for d in range(1, rows)], lambda distance: distance
    first = crossed(b_eff, 1, 2)
    second = crossed(b_eff, 2, 1)
    last = crossed(first, 2, 1)

    def place(distance):
        odd = lax.axis_index("col") & 1
        return jnp.where((distance == 0) | (distance == 3), distance, distance ^ (3 * odd))

    return [b_eff, first, second, last], place


def beside_kernel(*refs):
    *block_refs, out_ref = refs
    width = block_refs[0].shape[1]
    for i, block_ref in enumerate(block_refs):
        out_ref[:, i * width : (i + 1) * width] = block_ref[...]


def beside(blocks):
    rows, width = blocks[0].shape
    return pl.pallas_call(
        beside_kernel,
        out_shape=pltpu.VMEM((rows, width * len(blocks)), blocks[0].dtype),
        in_specs=[VMEM] * len(blocks),
        out_specs=VMEM,
        compiler_params=LIMITS,
        cost_estimate=cost(0, 4 * rows * width * len(blocks)),
    )(*(near(block) for block in blocks))


def started_early(block):
    return pl.pallas_call(
        lambda block_ref, same_ref: None,
        out_shape=pltpu.VMEM(block.shape, block.dtype),
        in_specs=[VMEM],
        out_specs=VMEM,
        input_output_aliases={0: 0},
        cost_estimate=cost(460_000_000, 0),
    )(near(block))


def gathered_a(a_eff):
    cols = lax.axis_size("col")
    blocks = {0: a_eff} | {d: swapped(a_eff, "col", d) for d in range(2, cols, 2)}
    if cols == 8:
        blocks[6] = started_early(blocks[6])
        groups = ((0, 4), (2, 6))
    else:
        groups = (tuple(blocks)[: cols // 4], tuple(blocks)[cols // 4 :])
    owns = [(beside([blocks[d] for d in group]), group) for group in groups]
    partners = [(swapped(own, "col", 1), tuple(d ^ 1 for d in group)) for own, group in owns]
    return owns, partners


def per_device(row_ids, a_tiles, a_mask, b_tiles, b_mask, c_keep):
    sizes = (lax.axis_size("row"), lax.axis_size("col"))
    assert sizes[1] == 2 * sizes[0] and b_tiles.shape[0] == 2 * a_tiles.shape[1]
    a_eff, b_eff = masked(a_tiles, a_mask, b_tiles, b_mask)
    b_blocks, b_place = gathered_b(b_eff)
    owns, partners = gathered_a(a_eff)
    total, tail, keep, firsts = early_product(
        row_ids, c_keep, owns, partners[0], b_blocks[:-1], b_place, sizes
    )
    return last_product(keep, total, tail, firsts, partners[1], b_blocks[-1], b_place, sizes)


def solution(mesh):
    placed = (
        P("row"),
        P("row", "col"),
        P("row", "col"),
        P("row", "col"),
        P("row", "col"),
        P(None, "col"),
    )
    return jax.shard_map(
        per_device, mesh=mesh, in_specs=placed, out_specs=P("row", "col"), check_vma=False
    )
```
